768 devices in a mesh: dp: 16 (over y, core), shard: 48 (over z, x).
Axes of the slice: x: 4, y: 8, z: 12, core: 2. Of those that a mesh axis runs over, the one named last changes fastest.
Arguments:
- grad: bfloat16 [768, 512, 512], P('shard', 'dp'), may hold values from -150 to 150
- owner: int32 [768], replicated, may hold values from 0 to 47, as said below
- left_root: bfloat16 [48, 32, 512, 512], P('shard', 'dp'), may hold values from -1 to 4
- right_root: bfloat16 [48, 32, 512, 512], P('shard', 'dp'), may hold values from -1 to 4
- momentum: float32 [768, 512, 512], P('shard', 'dp'), may hold values from -6 to 6
Outputs:
- new_momentum: float32 [768, 512, 512], P('shard', 'dp')
The draws below stay inside these ranges and needn't reach their ends.
Inputs may be any that keep to these rules, and one draw needn't show every extreme that they name: The 16 blocks of one source index (blocks s * 16 to s * 16 + 15) go to distinct owners; no owner index is given more than 32 blocks, and some owner index is given exactly 32 in every draw.
All inputs are finite; a program needn't handle non-finite values.
Results may differ from the reference program's by a relative error of at most 0.017.
Values may be sent and summed in bfloat16 or wider, within the bound.
A program may use at most 32 MiB of HBM per device.

```python
import math
import jax
import jax.numpy as jnp
from jax import lax

BLOCK = 512
NMAT = 4
MOST = 32
SRC_BLK = 16
NB = 768
N_SHARD = 48


def draw_owner(key, part):
    key = jax.random.fold_in(key, 3)
    key_perm, key_shift, key_flags = jax.random.split(key, 3)
    count = N_SHARD
    per_src = SRC_BLK
    labels = jax.random.permutation(key_perm, count).astype(jnp.int32)
    offset = jax.random.randint(key_shift, (), 0, count).astype(jnp.int32)
    flags = jax.random.randint(key_flags, (count // 4,), 0, 2).astype(jnp.int32)
    flags = flags.at[0].set(1)
    block_ids = jnp.arange(NB, dtype=jnp.int32)
    within = block_ids % per_src
    source = block_ids // per_src
    order = within * count + (source - offset) % count
    group = order // (4 * per_src)
    remain = order % (4 * per_src)
    halfk = per_src // 2
    sub_skew = (remain >= 2 * per_src).astype(jnp.int32) + (remain >= 3 * per_src).astype(jnp.int32) + (remain >= 3 * per_src + halfk).astype(jnp.int32)
    sub_even = (remain >= per_src).astype(jnp.int32) + (remain >= 2 * per_src).astype(jnp.int32) + (remain >= 3 * per_src).astype(jnp.int32)
    ranked = 4 * group + jnp.where(flags[group] == 1, sub_skew, sub_even)
    return labels[ranked].astype(jnp.int32)


def draw_grad(key, part):
    key = jax.random.fold_in(key, 5)
    key_base, key_row, key_col = jax.random.split(key, 3)
    shape = (NB, BLOCK, BLOCK)
    base = jnp.clip(jax.random.normal(key_base, shape, jnp.float32), -5.0, 5.0)
    spread = math.log(10.0)
    lowest = 0.3
    row_scale = lowest * jnp.exp(spread * jax.random.uniform(key_row, (NB, BLOCK, 1), jnp.float32))
    col_scale = lowest * jnp.exp(spread * jax.random.uniform(key_col, (NB, 1, BLOCK), jnp.float32))
    per_mat = NB // NMAT
    place = (jnp.arange(NB) % per_mat).astype(jnp.float32) / max(per_mat - 1, 1)
    ramp = jnp.exp(math.log(3.0) * place)[:, None, None]
    return (base * row_scale * col_scale * ramp).astype(jnp.bfloat16)


def off_diagonal(key, shape):
    raw = jnp.clip(jax.random.normal(key, shape, jnp.float32), -4.0, 4.0) * (0.6 / math.sqrt(BLOCK))
    return 0.5 * (raw + jnp.swapaxes(raw, -1, -2))


def slot_ramp():
    steps = jnp.arange(MOST).astype(jnp.float32) / max(MOST - 1, 1)
    return (0.5 * jnp.exp(math.log(5.0) * steps))[None, :, None, None]


def assemble(offpart, diag):
    rows_i = jnp.arange(BLOCK)[:, None]
    cols_j = jnp.arange(BLOCK)[None, :]
    unit = (rows_i == cols_j).astype(jnp.float32)
    whole = offpart * (1.0 - unit) + unit * diag[..., None]
    return (whole * slot_ramp()).astype(jnp.bfloat16)


def draw_left_root(key, part):
    key = jax.random.fold_in(key, 11)
    key_off, key_diag = jax.random.split(key)
    shape = (N_SHARD, MOST, BLOCK, BLOCK)
    diag = jnp.exp(math.log(1.5) * jax.random.uniform(key_diag, shape[:-1], jnp.float32))
    return assemble(off_diagonal(key_off, shape), diag)


def draw_right_root(key, part):
    key = jax.random.fold_in(key, 17)
    key_off, key_diag = jax.random.split(key)
    shape = (N_SHARD, MOST, BLOCK, BLOCK)
    diag = jnp.exp(math.log(1.5) * jax.random.uniform(key_diag, shape[:-1], jnp.float32))
    return assemble(off_diagonal(key_off, shape), diag)


def levels(own_key, shape, cuts, low, high):
    def one(axis_at, blocks):
        heights = jax.random.uniform(jax.random.fold_in(jax.random.fold_in(own_key, 6), axis_at), (blocks,), jnp.float32, low / len(cuts), high / len(cuts))
        return jnp.repeat(jnp.exp(heights), shape[axis_at] // blocks).reshape((-1,) + (1,) * (len(shape) - axis_at - 1))

    gain = one(*cuts[0])
    for cut in cuts[1:]:
        gain = gain * one(*cut)
    return gain


def gaussian(own_key, shape, scale, limit, cuts=(), kind=jnp.bfloat16):
    drawn = jax.random.normal(own_key, shape, jnp.float32) * scale
    if len(cuts) > 0:
        drawn = levels(own_key, shape, cuts, -0.22, 0.18) * drawn
    return jnp.clip(drawn, min=-limit, max=limit).astype(kind)


def setup_inputs(seed: int = 0) -> dict:
    streams_of = jax.random.split(jax.random.key(seed), 6)
    grad = draw_grad(jax.random.fold_in(streams_of[5], 71), 0)
    owner = draw_owner(jax.random.fold_in(streams_of[5], 71), 0)
    left_root = draw_left_root(jax.random.fold_in(streams_of[5], 71), 0)
    right_root = draw_right_root(jax.random.fold_in(streams_of[5], 71), 0)
    momentum = gaussian(streams_of[4], (NB, BLOCK, BLOCK), 1.0, 6.0, ((0, 48), (1, 16)), jnp.float32)
    return {"grad": grad, "owner": owner, "left_root": left_root, "right_root": right_root, "momentum": momentum}


EPS = 1e-06
BETA = 0.9

def reference(grad, owner, left_root, right_root, momentum):
    nblk = grad.shape[0]
    owners_iota = jnp.arange(N_SHARD, dtype=jnp.int32)
    hot = (owner[:, None] == owners_iota[None, :]).astype(jnp.int32)
    before = jnp.cumsum(hot, axis=0) - hot
    slot = lax.optimization_barrier(jnp.sum(before * hot, axis=1)).astype(jnp.int32)

    def one_block(index):
        holder = owner[index]
        place = slot[index]
        block = grad[index]
        half = jnp.dot(block, right_root[holder, place], preferred_element_type=jnp.float32).astype(jnp.bfloat16)
        precond = jnp.dot(left_root[holder, place], half, preferred_element_type=jnp.float32)
        wide = block.astype(jnp.float32)
        return (precond, jnp.sum(wide * wide), jnp.sum(precond * precond))
    precond, grad_terms, pre_terms = lax.map(one_block, jnp.arange(nblk, dtype=jnp.int32))
    per_mat = nblk // NMAT
    grad_sq = lax.optimization_barrier(jnp.sum(grad_terms.reshape(NMAT, per_mat), axis=1))
    pre_sq = lax.optimization_barrier(jnp.sum(pre_terms.reshape(NMAT, per_mat), axis=1))
    graft = jnp.sqrt(grad_sq / (pre_sq + EPS))
    update = (precond * jnp.repeat(graft, per_mat)[:, None, None]).astype(jnp.bfloat16)
    return BETA * momentum + update.astype(jnp.float32)
```

```python
import functools

import jax
import jax.numpy as jnp
from jax import lax
from jax.experimental import pallas as pl
from jax.experimental.pallas import tpu as pltpu
from jax.sharding import PartitionSpec as P

NMAT = 4
EPS = 1e-06
BETA = 0.9
LANES = 128
X_RING = 4


def route_tables(owner, n_shard, blocks, most):
    me = lax.axis_index("shard")
    ids = jnp.arange(n_shard, dtype=jnp.int32)
    mine = lax.dynamic_slice_in_dim(owner, me * blocks, blocks)
    ks = jnp.arange(blocks, dtype=jnp.int32)
    block_of = jnp.sum(jnp.where(mine[None, :] == ids[:, None], ks[None, :], 0), axis=1)
    here = jnp.sum((owner.reshape(n_shard, blocks) == me).astype(jnp.int32), axis=1)
    slot_of = jnp.sum(jnp.where(ids[None, :] < ids[:, None], here[None, :], 0), axis=1)
    slots = jnp.arange(most, dtype=jnp.int32)
    hit = (slot_of[None, :] == slots[:, None]) & (here[None, :] > 0)
    source_of = jnp.sum(jnp.where(hit, ids[None, :], 0), axis=1)
    slot_of = jnp.minimum(slot_of, most - 1)
    count = jnp.sum(here, keepdims=True)
    return jnp.concatenate([block_of, source_of, slot_of, mine, count])


def kernel(
    n_dp, n_shard, chunks,
    tab, grad, left_hbm, right_hbm, mom_hbm, out,
    send, pack, full, pre, send2, got, back, got2,
    left, right, mom, acc, half, dp_stat, x_stat, z_stat,
    load_sem, fs_send, fs_recv, fd_send, fd_recv, bd_send, bd_recv, bs_send, bs_recv,
    st_send, st_recv,
):
    blocks, rows, width = grad.shape
    cw = width // chunks
    own = left.shape[0]
    most = own * n_dp
    n_x = X_RING
    n_z = n_shard // n_x
    me_d = lax.axis_index("dp")
    me_s = lax.axis_index("shard")
    me_z = me_s // n_x
    me_x = me_s % n_x
    block_of = lambda o: tab[o]
    source_of = lambda j: tab[n_shard + j]
    slot_of = lambda s: tab[n_shard + most + s]
    owner_of = lambda k: tab[2 * n_shard + most + k]
    live_slots = tab[2 * n_shard + most + blocks]

    loads = [
        pltpu.make_async_copy(src, dst, load_sem.at[i])
        for i, (src, dst) in enumerate(((right_hbm, right), (left_hbm, left), (mom_hbm, mom)))
    ]
    for load in loads:
        load.start()

    barrier = pltpu.get_barrier_semaphore()

    def greet_shard(t, carry):
        pl.semaphore_signal(barrier, inc=1, device_id={"shard": (me_s + t) % n_shard})
        return carry

    def greet_dp(t, carry):
        pl.semaphore_signal(barrier, inc=1, device_id={"dp": (me_d + t) % n_dp})
        return carry

    lax.fori_loop(1, n_shard, greet_shard, 0)
    lax.fori_loop(1, n_dp, greet_dp, 0)

    def fill(o, carry):
        send[o] = grad[block_of(o)]
        return carry

    lax.fori_loop(0, n_shard, fill, 0, unroll=2)

    pl.semaphore_wait(barrier, n_shard - 1 + n_dp - 1)

    def send_shard(src, dst, c, send_sem, recv_sem):
        cols = pl.ds(c * cw, cw)

        def one(t, carry):
            to = (me_s + t) % n_shard
            pltpu.make_async_remote_copy(
                src_ref=src.at[to, :, cols], dst_ref=dst[c].at[me_s],
                send_sem=send_sem.at[c], recv_sem=recv_sem.at[c],
                device_id={"shard": to},
            ).start()
            return carry

        lax.fori_loop(1, n_shard, one, 0)
        dst[c][me_s] = src[me_s, :, c * cw:(c + 1) * cw]

    def wait_bytes(ref, sem):
        pltpu.make_async_copy(ref, ref, sem).wait()

    for c in range(chunks):
        send_shard(send, got, c, fs_send, fs_recv)

    lane = lax.broadcasted_iota(jnp.int32, (1, LANES), 1)
    my_mat = me_s // (n_shard // NMAT)
    wide = grad[...].astype(jnp.float32)
    grad_term = jnp.sum(wide * wide)

    for c in range(chunks):
        wait_bytes(got[c].at[pl.ds(0, n_shard - 1)], fs_recv.at[c])

        def compact(j, carry):
            pack[c, j] = got[c][source_of(j)]
            return carry

        lax.fori_loop(0, most, compact, 0, unroll=4)

        def to_holder(t, carry):
            to = (me_d + t) % n_dp
            pltpu.make_async_remote_copy(
                src_ref=pack.at[c, pl.ds(to * own, own)],
                dst_ref=full.at[c, :, pl.ds(me_d * rows, rows)],
                send_sem=fd_send.at[c], recv_sem=fd_recv.at[c],
                device_id={"dp": to},
            ).start()
            return carry

        lax.fori_loop(1, n_dp, to_holder, 0)
        full[c, :, pl.ds(me_d * rows, rows)] = pack[c, pl.ds(me_d * own, own)]

    loads[0].wait()
    for c in range(chunks):
        wait_bytes(full.at[c, :, pl.ds(0, (n_dp - 1) * rows)], fd_recv.at[c])
        for i in range(own):
            part = jnp.dot(
                full[c, i], right[i, c * cw:(c + 1) * cw, :], preferred_element_type=jnp.float32
            )
            if c > 0:
                part = acc[i] + part
            if c < chunks - 1:
                acc[i] = part
            else:
                half[i] = part.astype(jnp.bfloat16)

    loads[1].wait()
    terms = [jnp.zeros((1, 1), jnp.float32) for _ in range(own)]
    for c in range(chunks):
        for i in range(own):
            part = jnp.dot(
                left[i], half[i, :, c * cw:(c + 1) * cw], preferred_element_type=jnp.float32
            )
            terms[i] += jnp.sum(part * part, keepdims=True)
            pre[c, i] = part.astype(jnp.bfloat16)

        def to_rows(t, carry):
            to = (me_d + t) % n_dp
            pltpu.make_async_remote_copy(
                src_ref=pre.at[c, :, pl.ds(to * rows, rows)],
                dst_ref=back[c].at[pl.ds(me_d * own, own)],
                send_sem=bd_send.at[c], recv_sem=bd_recv.at[c],
                device_id={"dp": to},
            ).start()
            return carry

        lax.fori_loop(1, n_dp, to_rows, 0)
        back[c][pl.ds(me_d * own, own)] = pre[c, :, pl.ds(me_d * rows, rows)]

    stat = jnp.where(lane == my_mat, grad_term, 0.0)
    for i in range(own):
        j = me_d * own + i
        mat = source_of(j) // (n_shard // NMAT)
        stat += jnp.where((lane == NMAT + mat) & (j < live_slots), terms[i], 0.0)

    def share(buf, index, count, which, target):
        def one(t, carry):
            pltpu.make_async_remote_copy(
                src_ref=buf.at[index], dst_ref=buf.at[index],
                send_sem=st_send.at[which], recv_sem=st_recv.at[which],
                device_id=target((index + t) % count),
            ).start()
            return carry

        lax.fori_loop(1, count, one, 0)

    def collect(buf, count, which):
        wait_bytes(buf.at[pl.ds(0, count - 1)], st_recv.at[which])
        return jnp.sum(buf[...], axis=0)

    dp_stat[me_d] = stat
    share(dp_stat, me_d, n_dp, 0, lambda p: {"dp": p})

    for c in range(chunks):
        wait_bytes(back[c].at[pl.ds(0, most - own)], bd_recv.at[c])

        def scatter(s, carry):
            send2[s, :, c * cw:(c + 1) * cw] = back[c][slot_of(s)]
            return carry

        lax.fori_loop(0, n_shard, scatter, 0, unroll=4)
        send_shard(send2, got2, c, bs_send, bs_recv)
        if c == 0:
            x_stat[me_x] = collect(dp_stat, n_dp, 0)
            share(x_stat, me_x, n_x, 1, lambda p: {"shard": me_z * n_x + p})
        if c == chunks - 1:
            z_stat[me_z] = collect(x_stat, n_x, 1)
            share(z_stat, me_z, n_z, 2, lambda p: {"shard": p * n_x + me_x})

    loads[2].wait()
    total = collect(z_stat, n_z, 2)
    grad_sq = jnp.sum(jnp.where(lane == my_mat, total, 0.0), axis=1, keepdims=True)
    pre_sq = jnp.sum(jnp.where(lane == NMAT + my_mat, total, 0.0), axis=1, keepdims=True)
    graft = jnp.sqrt(grad_sq / (pre_sq + EPS))
    for c in range(chunks):
        wait_bytes(got2[c].at[pl.ds(0, n_shard - 1)], bs_recv.at[c])

        def finish(k, carry):
            cols = slice(c * cw, (c + 1) * cw)
            update = graft * got2[c][owner_of(k)].astype(jnp.float32)
            out[k, :, cols] = BETA * mom[k, :, cols] + update
            return carry

        lax.fori_loop(0, blocks, finish, 0, unroll=2)

    for c in range(chunks):
        wait_bytes(send.at[pl.ds(0, n_shard - 1), :, pl.ds(c * cw, cw)], fs_send.at[c])
        wait_bytes(pack.at[c, pl.ds(0, most - own)], fd_send.at[c])
        wait_bytes(pre.at[c, :, pl.ds(0, (n_dp - 1) * rows)], bd_send.at[c])
        wait_bytes(send2.at[pl.ds(0, n_shard - 1), :, pl.ds(c * cw, cw)], bs_send.at[c])
    for which, (buf, count) in enumerate(((dp_stat, n_dp), (x_stat, n_x), (z_stat, n_z))):
        wait_bytes(buf.at[pl.ds(0, count - 1)], st_send.at[which])


def body(grad, owner, left_root, right_root, momentum):
    n_dp, n_shard = lax.axis_size("dp"), lax.axis_size("shard")
    blocks, rows, width = grad.shape
    own = left_root.shape[1]
    most = own * n_dp
    side = left_root.shape[2]
    chunks = max(1, min(4, width // LANES))
    cw = width // chunks
    n_x = X_RING
    n_z = n_shard // n_x
    tab = route_tables(owner, n_shard, blocks, most)
    bf16, f32 = jnp.bfloat16, jnp.float32
    vmem = pl.BlockSpec(memory_space=pltpu.VMEM)
    hbm = pl.BlockSpec(memory_space=pl.ANY)
    dma = pltpu.SemaphoreType.DMA
    flops = 4 * own * side * side * side
    return pl.pallas_call(
        functools.partial(kernel, n_dp, n_shard, chunks),
        out_shape=jax.ShapeDtypeStruct(momentum.shape, f32),
        in_specs=[pl.BlockSpec(memory_space=pltpu.SMEM), vmem, hbm, hbm, hbm],
        out_specs=vmem,
        scratch_shapes=[
            pltpu.VMEM((n_shard, rows, width), bf16),
            pltpu.VMEM((chunks, most, rows, cw), bf16),
            pltpu.VMEM((chunks, own, side, cw), bf16),
            pltpu.VMEM((chunks, own, side, cw), bf16),
            pltpu.VMEM((n_shard, rows, width), bf16),
            [pltpu.VMEM((n_shard, rows, cw), bf16)] * chunks,
            [pltpu.VMEM((most, rows, cw), bf16)] * chunks,
            [pltpu.VMEM((n_shard, rows, cw), bf16)] * chunks,
            pltpu.VMEM((own, side, width), bf16),
            pltpu.VMEM((own, side, width), bf16),
            pltpu.VMEM(momentum.shape, f32),
            pltpu.VMEM((own, side, width), f32),
            pltpu.VMEM((own, side, width), bf16),
            pltpu.VMEM((n_dp, 1, LANES), f32),
            pltpu.VMEM((n_x, 1, LANES), f32),
            pltpu.VMEM((n_z, 1, LANES), f32),
            dma((3,)),
            dma((chunks,)), dma((chunks,)), dma((chunks,)), dma((chunks,)),
            dma((chunks,)), dma((chunks,)), dma((chunks,)), dma((chunks,)),
            dma((3,)), dma((3,)),
        ],
        compiler_params=pltpu.CompilerParams(
            collective_id=0, has_side_effects=True, vmem_limit_bytes=56 * 1024 * 1024
        ),
        cost_estimate=pl.CostEstimate(flops=flops, bytes_accessed=5 << 20, transcendentals=0),
    )(tab, grad, left_root[0], right_root[0], momentum)


def solution(mesh):
    placed = (
        P("shard", "dp", None),
        P(),
        P("shard", "dp", None, None),
        P("shard", "dp", None, None),
        P("shard", "dp", None),
    )
    return jax.shard_map(
        body, mesh=mesh, in_specs=placed, out_specs=P("shard", "dp", None), check_vma=False
    )
```

```python
import functools

import jax
import jax.numpy as jnp
from jax import lax
from jax.experimental import pallas as pl
from jax.experimental.pallas import tpu as pltpu
from jax.sharding import PartitionSpec as P

NMAT = 4
EPS = 1e-06
BETA = 0.9
LANES = 128
VMEM_LIMIT = 53 << 20
UNROLL_SEND = 1
UNROLL_MOVE = 2
X_RING = 4


def route_tables(owner, n_shard, blocks, most):
    me = lax.axis_index("shard")
    ids = jnp.arange(n_shard, dtype=jnp.int32)
    mine = lax.dynamic_slice_in_dim(owner, me * blocks, blocks)
    ks = jnp.arange(blocks, dtype=jnp.int32)
    block_of = jnp.sum(jnp.where(mine[None, :] == ids[:, None], ks[None, :], 0), axis=1)
    here = jnp.sum((owner.reshape(n_shard, blocks) == me).astype(jnp.int32), axis=1)
    slot_of = jnp.sum(jnp.where(ids[None, :] < ids[:, None], here[None, :], 0), axis=1)
    slots = jnp.arange(most, dtype=jnp.int32)
    hit = (slot_of[None, :] == slots[:, None]) & (here[None, :] > 0)
    source_of = jnp.sum(jnp.where(hit, ids[None, :], 0), axis=1)
    slot_of = jnp.minimum(slot_of, most - 1)
    count = jnp.sum(here, keepdims=True)
    return jnp.concatenate([block_of, source_of, slot_of, mine, count])


def kernel(
    n_dp, n_shard, spans_out, spans_back, parts_out, parts_back,
    tab, grad_hbm, left_hbm, right_hbm, update,
    grad, send, pack, full, pre, send2, got, back, got2,
    left, right, acc, half, dp_stat, x_stat, z_stat,
    load_sem, fs_send, fs_recv, fd_send, fd_recv, bd_send, bd_recv, bs_send, bs_recv,
    st_send, st_recv,
):
    blocks, rows, width = grad.shape
    own = left.shape[0]
    most = own * n_dp
    n_x = X_RING
    n_z = n_shard // n_x
    me_d = lax.axis_index("dp")
    me_s = lax.axis_index("shard")
    me_z = me_s // n_x
    me_x = me_s % n_x
    block_of = lambda o: tab[o]
    source_of = lambda j: tab[n_shard + j]
    slot_of = lambda s: tab[n_shard + most + s]
    owner_of = lambda k: tab[2 * n_shard + most + k]
    live_slots = tab[2 * n_shard + most + blocks]

    loads = [
        pltpu.make_async_copy(src, dst, load_sem.at[i])
        for i, (src, dst) in enumerate(((grad_hbm, grad), (right_hbm, right), (left_hbm, left)))
    ]
    for load in loads:
        load.start()

    barrier = pltpu.get_barrier_semaphore()

    def greet_shard(t, carry):
        pl.semaphore_signal(barrier, inc=1, device_id={"shard": (me_s + t) % n_shard})
        return carry

    def greet_dp(t, carry):
        pl.semaphore_signal(barrier, inc=1, device_id={"dp": (me_d + t) % n_dp})
        return carry

    lax.fori_loop(1, n_shard, greet_shard, 0)
    lax.fori_loop(1, n_dp, greet_dp, 0)

    loads[0].wait()

    def fill(o, carry):
        send[o] = grad[block_of(o)]
        return carry

    lax.fori_loop(0, n_shard, fill, 0, unroll=UNROLL_MOVE)

    pl.semaphore_wait(barrier, n_shard - 1 + n_dp - 1)

    def wait_bytes(ref, sem):
        pltpu.make_async_copy(ref, ref, sem).wait()

    def send_shard(src, dst, p, part, send_sem, recv_sem):
        span, r0, nr = part

        def one(t, carry):
            to = (me_s + t) % n_shard
            pltpu.make_async_remote_copy(
                src_ref=src.at[to, pl.ds(r0, nr), pl.ds(*span)], dst_ref=dst[p].at[me_s],
                send_sem=send_sem.at[p], recv_sem=recv_sem.at[p],
                device_id={"shard": to},
            ).start()
            return carry

        lax.fori_loop(1, n_shard, one, 0, unroll=UNROLL_SEND)
        dst[p][me_s] = src[me_s, r0:r0 + nr, pl.ds(*span)]

    for p, part in enumerate(parts_out):
        send_shard(send, got, p, part, fs_send, fs_recv)

    lane = lax.broadcasted_iota(jnp.int32, (1, LANES), 1)
    my_mat = me_s // (n_shard // NMAT)
    wide = grad[...].astype(jnp.float32)
    grad_term = jnp.sum(wide * wide)

    p_of = {span: i for i, span in enumerate(spans_out)}

    for p, (span, r0, nr) in enumerate(parts_out):
        wait_bytes(got[p].at[pl.ds(0, n_shard - 1)], fs_recv.at[p])

        def compact(j, carry):
            pack[j, r0:r0 + nr, pl.ds(*span)] = got[p][source_of(j)]
            return carry

        lax.fori_loop(0, most, compact, 0, unroll=UNROLL_MOVE)

        def to_holder(t, carry):
            to = (me_d + t) % n_dp
            pltpu.make_async_remote_copy(
                src_ref=pack.at[pl.ds(to * own, own), pl.ds(r0, nr), pl.ds(*span)],
                dst_ref=full[p_of[span]].at[:, pl.ds(me_d * rows + r0, nr)],
                send_sem=fd_send.at[p], recv_sem=fd_recv.at[p],
                device_id={"dp": to},
            ).start()
            return carry

        lax.fori_loop(1, n_dp, to_holder, 0, unroll=UNROLL_SEND)
        full[p_of[span]][:, pl.ds(me_d * rows + r0, nr)] = pack[
            pl.ds(me_d * own, own), r0:r0 + nr, pl.ds(*span)
        ]

    loads[1].wait()
    for c, span in enumerate(spans_out):
        for p, part in enumerate(parts_out):
            if part[0] == span:
                wait_bytes(full[c].at[:, pl.ds(0, (n_dp - 1) * part[2])], fd_recv.at[p])
        for i in range(own):
            term = jnp.dot(
                full[c][i], right[i, pl.ds(*span), :], preferred_element_type=jnp.float32
            )
            if c > 0:
                term = acc[i] + term
            if c < len(spans_out) - 1:
                acc[i] = term
            else:
                half[i] = term.astype(jnp.bfloat16)

    loads[2].wait()
    terms = [jnp.zeros((1, 1), jnp.float32) for _ in range(own)]

    def precondition(span):
        for i in range(own):
            term = jnp.dot(
                left[i], half[i, :, pl.ds(*span)], preferred_element_type=jnp.float32
            )
            terms[i] += jnp.sum(term * term, keepdims=True)
            pre[i, :, pl.ds(*span)] = term.astype(jnp.bfloat16)

    def send_rows(p):
        span, r0, nr = parts_back[p]

        def one(t, carry):
            to = (me_d + t) % n_dp
            pltpu.make_async_remote_copy(
                src_ref=pre.at[:, pl.ds(to * rows + r0, nr), pl.ds(*span)],
                dst_ref=back[p].at[pl.ds(me_d * own, own)],
                send_sem=bd_send.at[p], recv_sem=bd_recv.at[p],
                device_id={"dp": to},
            ).start()
            return carry

        lax.fori_loop(1, n_dp, one, 0, unroll=UNROLL_SEND)
        back[p][pl.ds(me_d * own, own)] = pre[
            :, pl.ds(me_d * rows + r0, nr), pl.ds(*span)
        ]

    def share(buf, index, count, which, target):
        def one(t, carry):
            pltpu.make_async_remote_copy(
                src_ref=buf.at[index], dst_ref=buf.at[index],
                send_sem=st_send.at[which], recv_sem=st_recv.at[which],
                device_id=target((index + t) % count),
            ).start()
            return carry

        lax.fori_loop(1, count, one, 0)

    def collect(buf, count, which):
        wait_bytes(buf.at[pl.ds(0, count - 1)], st_recv.at[which])
        return jnp.sum(buf[...], axis=0)

    precondition(spans_back[0])
    for p, part in enumerate(parts_back):
        if part[0] == spans_back[0]:
            send_rows(p)
    for span in spans_back[1:]:
        precondition(span)
    stat = jnp.where(lane == my_mat, grad_term, 0.0)
    for i in range(own):
        mat = source_of(me_d * own + i) // (n_shard // NMAT)
        stat += jnp.where((lane == NMAT + mat) & (me_d * own + i < live_slots), terms[i], 0.0)
    dp_stat[me_d] = stat
    share(dp_stat, me_d, n_dp, 0, lambda p: {"dp": p})
    for p, part in enumerate(parts_back):
        if part[0] != spans_back[0]:
            send_rows(p)

    last = len(parts_back) - 1
    for p, (span, r0, nr) in enumerate(parts_back):
        if p == last:
            z_stat[me_z] = collect(x_stat, n_x, 1)
            share(z_stat, me_z, n_z, 2, lambda p: {"shard": p * n_x + me_x})
        wait_bytes(back[p].at[pl.ds(0, most - own)], bd_recv.at[p])

        def scatter(s, carry):
            send2[s, r0:r0 + nr, pl.ds(*span)] = back[p][slot_of(s)]
            return carry

        lax.fori_loop(0, n_shard, scatter, 0, unroll=UNROLL_MOVE)
        send_shard(send2, got2, p, parts_back[p], bs_send, bs_recv)
        if p == max(0, last - 2):
            x_stat[me_x] = collect(dp_stat, n_dp, 0)
            share(x_stat, me_x, n_x, 1, lambda p: {"shard": me_z * n_x + p})

    total = collect(z_stat, n_z, 2)
    grad_sq = jnp.sum(jnp.where(lane == my_mat, total, 0.0), axis=1, keepdims=True)
    pre_sq = jnp.sum(jnp.where(lane == NMAT + my_mat, total, 0.0), axis=1, keepdims=True)
    graft = jnp.sqrt(grad_sq / (pre_sq + EPS))
    for p, (span, r0, nr) in enumerate(parts_back):
        wait_bytes(got2[p].at[pl.ds(0, n_shard - 1)], bs_recv.at[p])

        def finish(k, carry):
            scaled = graft * got2[p][owner_of(k)].astype(jnp.float32)
            update[k, r0:r0 + nr, pl.ds(*span)] = scaled.astype(jnp.bfloat16)
            return carry

        lax.fori_loop(0, blocks, finish, 0, unroll=UNROLL_MOVE)

    for p, (span, r0, nr) in enumerate(parts_out):
        area = pl.ds(r0, nr), pl.ds(*span)
        wait_bytes(send.at[(pl.ds(0, n_shard - 1), *area)], fs_send.at[p])
        wait_bytes(pack.at[(pl.ds(0, most - own), *area)], fd_send.at[p])
    for p, (span, r0, nr) in enumerate(parts_back):
        area = pl.ds(r0, nr), pl.ds(*span)
        wait_bytes(pre.at[:, pl.ds(0, (n_dp - 1) * nr), pl.ds(*span)], bd_send.at[p])
        wait_bytes(send2.at[(pl.ds(0, n_shard - 1), *area)], bs_send.at[p])
    for which, (buf, count) in enumerate(((dp_stat, n_dp), (x_stat, n_x), (z_stat, n_z))):
        wait_bytes(buf.at[pl.ds(0, count - 1)], st_send.at[which])


def body(grad, owner, left_root, right_root, momentum):
    n_dp, n_shard = lax.axis_size("dp"), lax.axis_size("shard")
    blocks, rows, width = grad.shape
    own = left_root.shape[1]
    most = own * n_dp
    side = left_root.shape[2]
    n_x = X_RING
    n_z = n_shard // n_x
    halves = ((0, rows // 2), (rows // 2, rows // 2))
    big = width - 2 * LANES
    spans_out = [(0, big)] if big else []
    spans_out += [(big, LANES), (big + LANES, LANES)]
    spans_back = [(0, LANES), (LANES, LANES)] + ([(2 * LANES, big)] if big else [])
    parts_out = [(span, 0, rows) for span in spans_out[:-1]]
    parts_out += [(spans_out[-1], *h) for h in halves]
    parts_back = [(spans_back[0], *h) for h in halves]
    parts_back += [(span, 0, rows) for span in spans_back[1:]]
    n_out, n_back = len(parts_out), len(parts_back)
    tab = route_tables(owner, n_shard, blocks, most)
    bf16, f32 = jnp.bfloat16, jnp.float32
    vmem = pl.BlockSpec(memory_space=pltpu.VMEM)
    hbm = pl.BlockSpec(memory_space=pl.ANY)
    dma = pltpu.SemaphoreType.DMA
    flops = 4 * own * side * side * side
    update = pl.pallas_call(
        functools.partial(kernel, n_dp, n_shard, spans_out, spans_back, parts_out, parts_back),
        out_shape=jax.ShapeDtypeStruct(grad.shape, bf16),
        in_specs=[pl.BlockSpec(memory_space=pltpu.SMEM), hbm, hbm, hbm],
        out_specs=vmem,
        scratch_shapes=[
            pltpu.VMEM(grad.shape, bf16),
            pltpu.VMEM((n_shard, rows, width), bf16),
            pltpu.VMEM((most, rows, width), bf16),
            [pltpu.VMEM((own, side, w), bf16) for _, w in spans_out],
            pltpu.VMEM((own, side, width), bf16),
            pltpu.VMEM((n_shard, rows, width), bf16),
            [pltpu.VMEM((n_shard, nr, span[1]), bf16) for span, _, nr in parts_out],
            [pltpu.VMEM((most, nr, span[1]), bf16) for span, _, nr in parts_back],
            [pltpu.VMEM((n_shard, nr, span[1]), bf16) for span, _, nr in parts_back],
            pltpu.VMEM((own, side, width), bf16),
            pltpu.VMEM((own, side, width), bf16),
            pltpu.VMEM((own, side, width), f32),
            pltpu.VMEM((own, side, width), bf16),
            pltpu.VMEM((n_dp, 1, LANES), f32),
            pltpu.VMEM((n_x, 1, LANES), f32),
            pltpu.VMEM((n_z, 1, LANES), f32),
            dma((3,)),
            dma((n_out,)), dma((n_out,)), dma((n_out,)), dma((n_out,)),
            dma((n_back,)), dma((n_back,)), dma((n_back,)), dma((n_back,)),
            dma((3,)), dma((3,)),
        ],
        compiler_params=pltpu.CompilerParams(
            collective_id=0, has_side_effects=True, vmem_limit_bytes=VMEM_LIMIT
        ),
        cost_estimate=pl.CostEstimate(flops=flops, bytes_accessed=5 << 20, transcendentals=0),
    )(tab, grad, left_root[0], right_root[0])
    return BETA * momentum + update.astype(f32)


def solution(mesh):
    placed = (
        P("shard", "dp", None),
        P(),
        P("shard", "dp", None, None),
        P("shard", "dp", None, None),
        P("shard", "dp", None),
    )
    return jax.shard_map(
        body, mesh=mesh, in_specs=placed, out_specs=P("shard", "dp", None), check_vma=False
    )
```

```python
import functools

import jax
import jax.numpy as jnp
from jax import lax
from jax.experimental import pallas as pl
from jax.experimental.pallas import tpu as pltpu
from jax.sharding import PartitionSpec as P

NMAT = 4
EPS = 1e-06
BETA = 0.9
LANES = 128
VMEM_LIMIT = 53 << 20
UNROLL_SEND = 1
UNROLL_MOVE = 2
X_RING = 4


def route_tables(owner, n_shard, blocks, most):
    me = lax.axis_index("shard")
    ids = jnp.arange(n_shard, dtype=jnp.int32)
    mine = lax.dynamic_slice_in_dim(owner, me * blocks, blocks)
    ks = jnp.arange(blocks, dtype=jnp.int32)
    block_of = jnp.sum(jnp.where(mine[None, :] == ids[:, None], ks[None, :], 0), axis=1)
    here = jnp.sum((owner.reshape(n_shard, blocks) == me).astype(jnp.int32), axis=1)
    slot_of = jnp.sum(jnp.where(ids[None, :] < ids[:, None], here[None, :], 0), axis=1)
    slots = jnp.arange(most, dtype=jnp.int32)
    hit = (slot_of[None, :] == slots[:, None]) & (here[None, :] > 0)
    source_of = jnp.sum(jnp.where(hit, ids[None, :], 0), axis=1)
    slot_of = jnp.minimum(slot_of, most - 1)
    count = jnp.sum(here, keepdims=True)
    return jnp.concatenate([block_of, source_of, slot_of, mine, count])


def kernel(
    n_dp, n_shard, spans_out, spans_back, parts_out, parts_back,
    tab, grad_hbm, left_hbm, right_hbm, update,
    grad, send, pack, full, pre, send2, got, back, got2,
    left, right, acc, half, dp_stat, x_stat, z_stat,
    load_sem, fs_send, fs_recv, fd_send, fd_recv, bd_send, bd_recv, bs_send, bs_recv,
    st_send, st_recv,
):
    blocks, rows, width = grad.shape
    own = left.shape[0]
    most = own * n_dp
    n_x = X_RING
    n_z = n_shard // n_x
    me_d = lax.axis_index("dp")
    me_s = lax.axis_index("shard")
    me_z = me_s // n_x
    me_x = me_s % n_x
    block_of = lambda o: tab[o]
    source_of = lambda j: tab[n_shard + j]
    slot_of = lambda s: tab[n_shard + most + s]
    owner_of = lambda k: tab[2 * n_shard + most + k]
    live_slots = tab[2 * n_shard + most + blocks]

    loads = [
        pltpu.make_async_copy(src, dst, load_sem.at[i])
        for i, (src, dst) in enumerate(((grad_hbm, grad), (right_hbm, right), (left_hbm, left)))
    ]
    for load in loads:
        load.start()

    barrier = pltpu.get_barrier_semaphore()

    def greet_shard(t, carry):
        pl.semaphore_signal(barrier, inc=1, device_id={"shard": (me_s + t) % n_shard})
        return carry

    def greet_dp(t, carry):
        pl.semaphore_signal(barrier, inc=1, device_id={"dp": (me_d + t) % n_dp})
        return carry

    lax.fori_loop(1, n_shard, greet_shard, 0)
    lax.fori_loop(1, n_dp, greet_dp, 0)

    loads[0].wait()

    def fill(o, carry):
        send[o] = grad[block_of(o)]
        return carry

    lax.fori_loop(0, n_shard, fill, 0, unroll=UNROLL_MOVE)

    pl.semaphore_wait(barrier, n_shard - 1 + n_dp - 1)

    def wait_bytes(ref, sem):
        pltpu.make_async_copy(ref, ref, sem).wait()

    def send_shard(src, dst, p, part, send_sem, recv_sem):
        span, r0, nr = part

        def one(t, carry):
            u = n_shard - t
            hop = u // n_x
            dz = ((hop + 1) // 2) * (2 * (hop % 2) - 1)
            to = (me_z + dz + n_z) % n_z * n_x + (me_x + u) % n_x
            pltpu.make_async_remote_copy(
                src_ref=src.at[to, pl.ds(r0, nr), pl.ds(*span)], dst_ref=dst[p].at[me_s],
                send_sem=send_sem.at[p], recv_sem=recv_sem.at[p],
                device_id={"shard": to},
            ).start()
            return carry

        lax.fori_loop(1, n_shard, one, 0, unroll=UNROLL_SEND)
        dst[p][me_s] = src[me_s, r0:r0 + nr, pl.ds(*span)]

    for p, part in enumerate(parts_out):
        send_shard(send, got, p, part, fs_send, fs_recv)

    lane = lax.broadcasted_iota(jnp.int32, (1, LANES), 1)
    my_mat = me_s // (n_shard // NMAT)
    wide = grad[...].astype(jnp.float32)
    grad_term = jnp.sum(wide * wide)

    p_of = {span: i for i, span in enumerate(spans_out)}

    for p, (span, r0, nr) in enumerate(parts_out):
        wait_bytes(got[p].at[pl.ds(0, n_shard - 1)], fs_recv.at[p])

        def compact(j, carry):
            pack[j, r0:r0 + nr, pl.ds(*span)] = got[p][source_of(j)]
            return carry

        lax.fori_loop(0, most, compact, 0, unroll=UNROLL_MOVE)

        def to_holder(t, carry):
            to = (me_d + t) % n_dp
            pltpu.make_async_remote_copy(
                src_ref=pack.at[pl.ds(to * own, own), pl.ds(r0, nr), pl.ds(*span)],
                dst_ref=full[p_of[span]].at[:, pl.ds(me_d * rows + r0, nr)],
                send_sem=fd_send.at[p], recv_sem=fd_recv.at[p],
                device_id={"dp": to},
            ).start()
            return carry

        lax.fori_loop(1, n_dp, to_holder, 0, unroll=UNROLL_SEND)
        full[p_of[span]][:, pl.ds(me_d * rows + r0, nr)] = pack[
            pl.ds(me_d * own, own), r0:r0 + nr, pl.ds(*span)
        ]

    loads[1].wait()
    for c, span in enumerate(spans_out):
        for p, part in enumerate(parts_out):
            if part[0] == span:
                wait_bytes(full[c].at[:, pl.ds(0, (n_dp - 1) * part[2])], fd_recv.at[p])
        for i in range(own):
            term = jnp.dot(
                full[c][i], right[i, pl.ds(*span), :], preferred_element_type=jnp.float32
            )
            if c > 0:
                term = acc[i] + term
            if c < len(spans_out) - 1:
                acc[i] = term
            else:
                half[i] = term.astype(jnp.bfloat16)

    loads[2].wait()
    terms = [jnp.zeros((1, 1), jnp.float32) for _ in range(own)]

    def precondition(span):
        for i in range(own):
            term = jnp.dot(
                left[i], half[i, :, pl.ds(*span)], preferred_element_type=jnp.float32
            )
            terms[i] += jnp.sum(term * term, keepdims=True)
            pre[i, :, pl.ds(*span)] = term.astype(jnp.bfloat16)

    def send_rows(p):
        span, r0, nr = parts_back[p]

        def one(t, carry):
            to = (me_d + t) % n_dp
            pltpu.make_async_remote_copy(
                src_ref=pre.at[:, pl.ds(to * rows + r0, nr), pl.ds(*span)],
                dst_ref=back[p].at[pl.ds(me_d * own, own)],
                send_sem=bd_send.at[p], recv_sem=bd_recv.at[p],
                device_id={"dp": to},
            ).start()
            return carry

        lax.fori_loop(1, n_dp, one, 0, unroll=UNROLL_SEND)
        back[p][pl.ds(me_d * own, own)] = pre[
            :, pl.ds(me_d * rows + r0, nr), pl.ds(*span)
        ]

    def share(buf, index, count, which, target):
        def one(t, carry):
            pltpu.make_async_remote_copy(
                src_ref=buf.at[index], dst_ref=buf.at[index],
                send_sem=st_send.at[which], recv_sem=st_recv.at[which],
                device_id=target((index + t) % count),
            ).start()
            return carry

        lax.fori_loop(1, count, one, 0)

    def collect(buf, count, which):
        wait_bytes(buf.at[pl.ds(0, count - 1)], st_recv.at[which])
        return jnp.sum(buf[...], axis=0)

    precondition(spans_back[0])
    for p, part in enumerate(parts_back):
        if part[0] == spans_back[0]:
            send_rows(p)
    for span in spans_back[1:]:
        precondition(span)
    stat = jnp.where(lane == my_mat, grad_term, 0.0)
    for i in range(own):
        mat = source_of(me_d * own + i) // (n_shard // NMAT)
        stat += jnp.where((lane == NMAT + mat) & (me_d * own + i < live_slots), terms[i], 0.0)
    dp_stat[me_d] = stat
    share(dp_stat, me_d, n_dp, 0, lambda p: {"dp": p})
    for p, part in enumerate(parts_back):
        if part[0] != spans_back[0]:
            send_rows(p)

    last = len(parts_back) - 1
    for p, (span, r0, nr) in enumerate(parts_back):
        if p == last:
            z_stat[me_z] = collect(x_stat, n_x, 1)
            share(z_stat, me_z, n_z, 2, lambda p: {"shard": p * n_x + me_x})
        wait_bytes(back[p].at[pl.ds(0, most - own)], bd_recv.at[p])

        def scatter(s, carry):
            send2[s, r0:r0 + nr, pl.ds(*span)] = back[p][slot_of(s)]
            return carry

        lax.fori_loop(0, n_shard, scatter, 0, unroll=UNROLL_MOVE)
        send_shard(send2, got2, p, parts_back[p], bs_send, bs_recv)
        if p == max(0, last - 2):
            x_stat[me_x] = collect(dp_stat, n_dp, 0)
            share(x_stat, me_x, n_x, 1, lambda p: {"shard": me_z * n_x + p})

    total = collect(z_stat, n_z, 2)
    grad_sq = jnp.sum(jnp.where(lane == my_mat, total, 0.0), axis=1, keepdims=True)
    pre_sq = jnp.sum(jnp.where(lane == NMAT + my_mat, total, 0.0), axis=1, keepdims=True)
    graft = jnp.sqrt(grad_sq / (pre_sq + EPS))
    for p, (span, r0, nr) in enumerate(parts_back):
        wait_bytes(got2[p].at[pl.ds(0, n_shard - 1)], bs_recv.at[p])

        def finish(k, carry):
            scaled = graft * got2[p][owner_of(k)].astype(jnp.float32)
            update[k, r0:r0 + nr, pl.ds(*span)] = scaled.astype(jnp.bfloat16)
            return carry

        lax.fori_loop(0, blocks, finish, 0, unroll=UNROLL_MOVE)

    for p, (span, r0, nr) in enumerate(parts_out):
        area = pl.ds(r0, nr), pl.ds(*span)
        wait_bytes(send.at[(pl.ds(0, n_shard - 1), *area)], fs_send.at[p])
        wait_bytes(pack.at[(pl.ds(0, most - own), *area)], fd_send.at[p])
    for p, (span, r0, nr) in enumerate(parts_back):
        area = pl.ds(r0, nr), pl.ds(*span)
        wait_bytes(pre.at[:, pl.ds(0, (n_dp - 1) * nr), pl.ds(*span)], bd_send.at[p])
        wait_bytes(send2.at[(pl.ds(0, n_shard - 1), *area)], bs_send.at[p])
    for which, (buf, count) in enumerate(((dp_stat, n_dp), (x_stat, n_x), (z_stat, n_z))):
        wait_bytes(buf.at[pl.ds(0, count - 1)], st_send.at[which])


def body(grad, owner, left_root, right_root, momentum):
    n_dp, n_shard = lax.axis_size("dp"), lax.axis_size("shard")
    blocks, rows, width = grad.shape
    own = left_root.shape[1]
    most = own * n_dp
    side = left_root.shape[2]
    n_x = X_RING
    n_z = n_shard // n_x
    halves = ((0, rows // 2), (rows // 2, rows // 2))
    big = width - 2 * LANES
    spans_out = [(0, big)] if big else []
    spans_out += [(big, LANES), (big + LANES, LANES)]
    spans_back = [(0, LANES), (LANES, LANES)] + ([(2 * LANES, big)] if big else [])
    parts_out = [(span, 0, rows) for span in spans_out[:-1]]
    parts_out += [(spans_out[-1], *h) for h in halves]
    parts_back = [(spans_back[0], *h) for h in halves]
    parts_back += [(span, 0, rows) for span in spans_back[1:]]
    n_out, n_back = len(parts_out), len(parts_back)
    tab = route_tables(owner, n_shard, blocks, most)
    bf16, f32 = jnp.bfloat16, jnp.float32
    vmem = pl.BlockSpec(memory_space=pltpu.VMEM)
    hbm = pl.BlockSpec(memory_space=pl.ANY)
    dma = pltpu.SemaphoreType.DMA
    flops = 4 * own * side * side * side
    update = pl.pallas_call(
        functools.partial(kernel, n_dp, n_shard, spans_out, spans_back, parts_out, parts_back),
        out_shape=jax.ShapeDtypeStruct(grad.shape, bf16),
        in_specs=[pl.BlockSpec(memory_space=pltpu.SMEM), hbm, hbm, hbm],
        out_specs=vmem,
        scratch_shapes=[
            pltpu.VMEM(grad.shape, bf16),
            pltpu.VMEM((n_shard, rows, width), bf16),
            pltpu.VMEM((most, rows, width), bf16),
            [pltpu.VMEM((own, side, w), bf16) for _, w in spans_out],
            pltpu.VMEM((own, side, width), bf16),
            pltpu.VMEM((n_shard, rows, width), bf16),
            [pltpu.VMEM((n_shard, nr, span[1]), bf16) for span, _, nr in parts_out],
            [pltpu.VMEM((most, nr, span[1]), bf16) for span, _, nr in parts_back],
            [pltpu.VMEM((n_shard, nr, span[1]), bf16) for span, _, nr in parts_back],
            pltpu.VMEM((own, side, width), bf16),
            pltpu.VMEM((own, side, width), bf16),
            pltpu.VMEM((own, side, width), f32),
            pltpu.VMEM((own, side, width), bf16),
            pltpu.VMEM((n_dp, 1, LANES), f32),
            pltpu.VMEM((n_x, 1, LANES), f32),
            pltpu.VMEM((n_z, 1, LANES), f32),
            dma((3,)),
            dma((n_out,)), dma((n_out,)), dma((n_out,)), dma((n_out,)),
            dma((n_back,)), dma((n_back,)), dma((n_back,)), dma((n_back,)),
            dma((3,)), dma((3,)),
        ],
        compiler_params=pltpu.CompilerParams(
            collective_id=0, has_side_effects=True, vmem_limit_bytes=VMEM_LIMIT
        ),
        cost_estimate=pl.CostEstimate(flops=flops, bytes_accessed=5 << 20, transcendentals=0),
    )(tab, grad, left_root[0], right_root[0])
    return BETA * momentum + update.astype(f32)


def solution(mesh):
    placed = (
        P("shard", "dp", None),
        P(),
        P("shard", "dp", None, None),
        P("shard", "dp", None, None),
        P("shard", "dp", None),
    )
    return jax.shard_map(
        body, mesh=mesh, in_specs=placed, out_specs=P("shard", "dp", None), check_vma=False
    )
```
